128 devices in a mesh: row: 16 (over x, y), col: 8 (over z, core).
Axes of the slice: x: 4, y: 4, z: 4, core: 2. Of those that a mesh axis runs over, the one named last changes fastest.
Arguments:
- out_grad: bfloat16 [16384, 2880], P(('row', 'col')), may hold values from -6 to 6
- tokens: bfloat16 [16384, 2880], P(('row', 'col')), may hold values from -6 to 6
- expert_ids: int32 [16384, 4], P(('row', 'col')), may hold values from 0 to 127, all different within a row; in each aligned block of 128 rows (0 to 127, 128 to 255, ...) at most 5 rows name the same one
- gates: float32 [16384, 4], P(('row', 'col')), may hold values from 0.05 to 1
- w_gate_up: bfloat16 [128, 2880, 2880], P(('row', 'col')), may hold values from -0.109375 to 0.109375
- w_down: bfloat16 [128, 1440, 2880], P(('row', 'col')), may hold values from -0.15625 to 0.15625
Outputs:
- input_grad: bfloat16 [16384, 2880], P(('row', 'col'))
- route_grad: float32 [16384, 4], P(('row', 'col'))
The draws below stay inside these ranges and needn't reach their ends.
Inputs may be any that keep to these rules, and one draw needn't show every extreme that they name: `expert_ids`: A token's 4 experts differ; among the tokens of one device no expert is named more than 5 times, and in some device some expert is named exactly 5 times.
All inputs are finite; a program needn't handle non-finite values.
Results may differ from the reference program's by a relative error of at most 0.008.
Values may be sent and summed in bfloat16 or wider, within the bound.
A program may use at most 128 MiB of HBM per device.

```python
import math
import jax
import jax.numpy as jnp
import numpy as np
from jax import lax

D = 2880
FF = 1440
TOPK = 4
TOK_DEV = 128
EXPERTS = 128
TOKENS = 16384
CAP = 5
N_ROW = 16
N_COL = 8


def block_scale(key, shape, split, smallest, top_value):
    level, own = 1.0, jax.random.fold_in(key, 6)
    for position, parts in split:
        steps = jnp.exp(jax.random.uniform(jax.random.fold_in(own, position), (parts,), jnp.float32, smallest / len(split), top_value / len(split)))
        level = level * jnp.repeat(steps, shape[position] // parts).reshape([-1 if axis == position else 1 for axis in range(len(shape))])
    return level


def assign_block(own_key, own, number, rows, number_of, top, bound, lean):
    sequence = jax.random.permutation(own_key, number_of)
    heavy_load, usual = shares(number_of, rows * top, bound, lean, True), shares(number_of, rows * top, bound, lean, False)
    places = jnp.arange(number_of)

    def named(tallies, turn):
        used = int((tallies > 0).sum())
        fixed = max(1, used // 4)
        passed = fixed + (places - fixed + turn * (used - fixed)) % max(1, number_of - fixed)
        return jnp.zeros((number_of,), jnp.int32).at[sequence[jnp.where(places < fixed, places, passed)]].set(jnp.asarray(tallies, jnp.int32))

    tallies = jnp.where(number % 4 == 0, named(heavy_load, number // 4), named(usual, number - number // 4 - 1))
    mixed = jax.random.permutation(jax.random.fold_in(own, 3), number_of)
    source_of, receiver = mixed[0:number_of // 2 * 2:2], mixed[1:number_of // 2 * 2:2]
    slack = jnp.minimum(tallies[source_of] - 1, bound - tallies[receiver]) // 2
    slack = jnp.where((source_of == sequence[0]) | (receiver == sequence[0]) | (tallies[receiver] == 0), 0, jnp.maximum(slack, 0))
    passed = jax.random.randint(jax.random.fold_in(own, 4), (number_of // 2,), 0, 1 << 20) % (slack + 1)
    tallies = tallies.at[source_of].add(-passed).at[receiver].add(passed)
    members = jnp.searchsorted(jnp.cumsum(tallies), jnp.arange(rows * top), side="right").astype(jnp.int32)
    listing = members.reshape(top, rows).T
    listing = listing[jax.random.permutation(jax.random.fold_in(own, 1), rows)]
    turn = jax.random.randint(jax.random.fold_in(own, 2), (rows, 1), 0, top)
    return jnp.take_along_axis(listing, (jnp.arange(top)[None, :] + turn) % top, axis=1)


def shares(count, total, most, lean, full):
    weights = [(1 << 20) // math.isqrt(rank ** lean) + 1 for rank in range(1, count + 1)]
    largest = most if full else min(most, max(-(-total // count), total * weights[0] // sum(weights)))
    least = 1 if total - largest >= count - 1 else 0
    given, surplus = [largest] + [least] * (count - 1), total - largest - least * (count - 1)
    while surplus > 0:
        candidates = [i for i in range(1, count) if given[i] < largest] or [i for i in range(1, count) if given[i] < most]
        mass, left = sum([weights[i] for i in candidates]), surplus
        for i in candidates:
            extra = min(most - given[i], max(1, left * weights[i] // mass), surplus)
            given[i] = given[i] + extra
            surplus = surplus - extra
    return np.array(given)


def centred(stream_key, dims, spread, bound, split=(), kind=jnp.bfloat16):
    array = jax.random.normal(stream_key, dims, jnp.float32) * spread
    if len(split) > 0:
        array = block_scale(stream_key, dims, split, -0.22, 0.18) * array
    return jnp.clip(array, min=-bound, max=bound).astype(kind)


def setup_inputs(seed: int = 0) -> dict:
    key_of = jax.random.split(jax.random.key(seed), 7)
    out_grad = centred(key_of[0], (TOKENS, D), 1.0, 6.0, ((0, 128),))
    tokens = centred(key_of[1], (TOKENS, D), 1.0, 6.0, ((0, 128),))
    expert_ids_keys = jax.random.split(jax.random.fold_in(key_of[2], 1), TOKENS // TOK_DEV)
    expert_ids_turns = jax.random.permutation(jax.random.fold_in(key_of[2], 3), TOKENS // TOK_DEV)
    expert_ids = jax.vmap(lambda own, number: assign_block(jax.random.fold_in(key_of[2], 2), own, number, TOK_DEV, EXPERTS, TOPK, CAP, 1))(expert_ids_keys, expert_ids_turns).reshape((TOKENS, TOPK))
    gates = jnp.clip(0.05 + 0.95 * jax.random.uniform(key_of[3], (TOKENS, TOPK), jnp.float32) ** block_scale(key_of[3], (TOKENS, TOPK), ((0, 128),), -0.2, 0.2), 0.05, 1.0)
    w_gate_up = centred(key_of[4], (EXPERTS, D, 2 * FF), D ** -0.5, 0.109375, ((0, 128),))
    w_down = centred(key_of[5], (EXPERTS, FF, D), FF ** -0.5, 0.15625, ((0, 128),))
    return {"out_grad": out_grad, "tokens": tokens, "expert_ids": expert_ids, "gates": gates, "w_gate_up": w_gate_up, "w_down": w_down}


swish_alpha = 1.702


def expert_terms(grad_rows, input_rows, gate_up, down_proj):
    projected = jnp.dot(input_rows, gate_up, preferred_element_type=jnp.float32)
    gate_pre = projected[:, :FF]
    up_pre = projected[:, FF:]
    hidden_grad = jnp.dot(grad_rows, down_proj.T, preferred_element_type=jnp.float32)
    sigmoid_gate = jax.nn.sigmoid(swish_alpha * gate_pre)
    activated = gate_pre * sigmoid_gate
    hidden = (up_pre + 1.0) * activated
    route_term = jnp.sum(hidden_grad * hidden, axis=1)
    gate_grad = hidden_grad * (up_pre + 1.0) * sigmoid_gate * (1.0 + swish_alpha * gate_pre * (1.0 - sigmoid_gate))
    up_grad = hidden_grad * activated
    pre_grad = jnp.concatenate([gate_grad, up_grad], axis=1).astype(jnp.bfloat16)
    part_grad = jnp.dot(pre_grad, gate_up.T, preferred_element_type=jnp.float32).astype(jnp.bfloat16)
    return part_grad, route_term


def reference(out_grad, tokens, expert_ids, gates, w_gate_up, w_down):
    flat_ids = expert_ids.reshape(-1).astype(jnp.int32)
    sorted_rows = jnp.argsort(flat_ids, stable=True).astype(jnp.int32)
    counts = jnp.bincount(flat_ids, length=EXPERTS).astype(jnp.int32)
    starts = (jnp.cumsum(counts) - counts).astype(jnp.int32)
    most_rows = CAP * N_ROW * N_COL
    padded_rows = jnp.concatenate([sorted_rows, jnp.zeros((most_rows,), jnp.int32)])
    flat_gates = gates.reshape(-1)

    def expert_step(carry, expert):
        mixed_sum, route_sum = carry
        pick_index = lax.dynamic_slice_in_dim(padded_rows, starts[expert], most_rows)
        is_live = jnp.arange(most_rows, dtype=jnp.int32) < counts[expert]
        token_index = (pick_index // TOPK).astype(jnp.int32)
        part_grad, route_term = expert_terms(out_grad[token_index], tokens[token_index], w_gate_up[expert], w_down[expert])
        weight = jnp.where(is_live, flat_gates[pick_index], 0.0)
        mixed_sum = mixed_sum.at[token_index].add(weight[:, None] * part_grad.astype(jnp.float32))
        route_sum = route_sum.at[pick_index].add(jnp.where(is_live, route_term, 0.0))
        return (mixed_sum, route_sum), None

    start_carry = (jnp.zeros((TOKENS, D), jnp.float32), jnp.zeros((TOKENS * TOPK,), jnp.float32))
    (mixed_sum, route_sum), _ = lax.scan(expert_step, start_carry, jnp.arange(EXPERTS, dtype=jnp.int32))
    return mixed_sum.astype(jnp.bfloat16), route_sum.reshape(TOKENS, TOPK)
```

```python
import functools

import jax
import jax.numpy as jnp
from jax import lax
from jax.experimental import pallas as pl
from jax.experimental.pallas import tpu as pltpu
from jax.sharding import PartitionSpec as P

MESH = pl.DeviceIdType.MESH
BF = jnp.bfloat16
F32 = jnp.float32

swish_alpha = 1.702

DEVICES = 128
TOK = 128
ROUTES = 4
WIDTH = 2880
UNITS = 1440
WIRE = 1920
BACK = 1024
CHUNKS = 4
PER = DEVICES // CHUNKS
ROWS = PER * 16
GROUPS = PER // 16
M = PER * 5
WIDE = 1536


def dot(a, b):
    return jnp.dot(a, b, preferred_element_type=F32)


def dot_nt(a, b):
    return lax.dot_general(a, b, (((1,), (1,)), ((), ())), preferred_element_type=F32)


def iota(shape, axis):
    return lax.broadcasted_iota(jnp.int32, shape, axis)


def peer(place, sign):
    row, col = lax.axis_index("row"), lax.axis_index("col")
    step = place % 64
    a, b, c = step % 4, (step // 4) % 4, step // 16
    dx, dy, dz, dc = a, (a + b) % 4, (a + c) % 4, place // 64
    x = (row // 4 + sign * dx + 4) % 4
    y = (row % 4 + sign * dy + 4) % 4
    z = (col // 2 + sign * dz + 4) % 4
    core = (col % 2 + dc) % 2
    return (x * 4 + y, z * 2 + core)


def places_of(experts):
    row, col = lax.axis_index("row"), lax.axis_index("col")
    dx = ((experts >> 5) - row // 4) & 3
    dy = ((experts >> 3) - row % 4) & 3
    dz = ((experts >> 1) - col // 2) & 3
    dc = (experts - col % 2) & 1
    return dc * 64 + ((dz - dx) & 3) * 16 + ((dy - dx) & 3) * 4 + dx


def wire_row(r):
    q = r & 15
    part = (q * 13) >> 6
    return part, q - 5 * part + 1


def kernel(
    ids_ref, gates_ref, grad_ref, tok_ref, wgu_hbm, wd_hbm,
    out_ref, route_ref,
    wgu, wd, xs, slot_tp, gate_tp, sbuf, rbuf, psend, precv, gl, tl, proj, hg, pg, pst, acc, racc,
    wsem, ssem, rsem, pssem, prsem,
):
    load_gu = pltpu.make_async_copy(wgu_hbm.at[0], wgu, wsem.at[0])
    load_d = pltpu.make_async_copy(wd_hbm.at[0], wd, wsem.at[1])
    load_gu.start()
    load_d.start()

    barrier = pltpu.get_barrier_semaphore()

    @pl.loop(1, DEVICES)
    def _(p):
        pl.semaphore_signal(barrier, inc=1, device_id=peer(p, 1), device_id_type=MESH)

    places = places_of(ids_ref[...])
    lanes = iota((TOK, DEVICES), 1)
    chosen = jnp.zeros((TOK, DEVICES), F32)
    weight = jnp.zeros((TOK, DEVICES), F32)
    for k in range(ROUTES):
        hit = places[:, k : k + 1] == lanes
        chosen = jnp.where(hit, 1.0, chosen)
        weight = jnp.where(hit, gates_ref[:, k : k + 1], weight)
    earlier = (iota((TOK, TOK), 1) < iota((TOK, TOK), 0)).astype(F32).astype(BF)
    taken = dot(earlier, chosen.astype(BF))
    slot_tp[...] = (chosen * (taken + 1.0)).astype(BF)
    gate_tp[...] = weight.astype(BF)

    xs[0:128, :] = grad_ref[:, 0:1920]
    xs[128:256, :] = tok_ref[:, 0:1920]
    xs[256:384, 0:896] = grad_ref[:, 1920:2816]
    xs[256:384, 896:1792] = tok_ref[:, 1920:2816]
    low = (iota((64, 128), 0) == iota((64, 128), 1)).astype(F32).astype(BF)
    high = (iota((64, 128), 0) + 64 == iota((64, 128), 1)).astype(F32).astype(BF)
    xs[256:384, 1792:1920] = (
        dot(grad_ref[:, 2816:2880], low) + dot(tok_ref[:, 2816:2880], high)
    ).astype(BF)

    def pack(c):
        for g in range(ROWS // 256):
            base = c * ROWS + g * 256
            r = iota((256, 128), 0)
            spread = (iota((256, 128), 1) == c * PER + g * 16 + (r >> 4)).astype(F32).astype(BF)
            slots = dot_nt(spread, slot_tp[...])
            part, slot = wire_row(r)
            match = slots == slot.astype(F32)
            pick = jnp.concatenate(
                [jnp.where(match & (part == j), 1.0, 0.0).astype(BF) for j in range(3)], axis=1
            )

            @pl.loop(0, 5)
            def _(n):
                cols = pl.ds(pl.multiple_of(n * 384, 128), 384)
                sbuf[pl.ds(pl.multiple_of(base, 256), 256), cols] = dot(pick, xs[:, cols]).astype(BF)

    def forward(p, c):
        rows = pl.ds(pl.multiple_of(p * 16, 16), 16)
        return pltpu.make_async_remote_copy(
            src_ref=sbuf.at[rows], dst_ref=rbuf.at[rows],
            send_sem=ssem.at[c], recv_sem=rsem.at[c],
            device_id=peer(p, 1), device_id_type=MESH,
        )

    def backward(p, c):
        rows = pl.ds(pl.multiple_of(p * 16, 16), 16)
        return pltpu.make_async_remote_copy(
            src_ref=psend.at[rows], dst_ref=precv.at[rows],
            send_sem=pssem.at[c], recv_sem=prsem.at[c],
            device_id=peer(p, -1), device_id_type=MESH,
        )

    pack(0)
    pl.semaphore_wait(barrier, DEVICES - 1)
    pltpu.make_async_copy(sbuf.at[0:16], rbuf.at[0:16], rsem.at[0]).start()

    @pl.loop(1, PER)
    def _(p):
        forward(p, 0).start()

    @pl.loop(1, CHUNKS)
    def _(c):
        pack(c)

        @pl.loop(0, PER)
        def _(i):
            forward(c * PER + i, c).start()

    pst[...] = jnp.zeros_like(pst)
    acc[...] = jnp.zeros_like(acc)
    racc[...] = jnp.zeros_like(racc)
    load_gu.wait()
    load_d.wait()

    def chunk_rows(c):
        return pl.ds(pl.multiple_of(c * ROWS, 16), ROWS)

    @pl.loop(0, CHUNKS)
    def _(c):
        rows = chunk_rows(c)
        pltpu.make_async_copy(sbuf.at[rows], rbuf.at[rows], rsem.at[c]).wait()

        part, slot = wire_row(iota((240, 256), 1))
        target = part * 80 + (iota((240, 256), 1) >> 4) * 5 + slot - 1
        sort = ((target == iota((240, 256), 0)) & (part < 3)).astype(F32).astype(BF)
        down = (iota((128, 128), 0) == iota((128, 128), 1) + 64).astype(F32).astype(BF)
        for g in range(GROUPS):
            src = pl.ds(pl.multiple_of(c * ROWS + g * 256, 256), 256)
            dst = slice(g * 80, g * 80 + 80)
            for n0, n1 in ((0, 256), (256, 512), (512, 896), (896, 1152), (1152, 1408), (1408, 1792), (1792, 1920)):
                got = dot(sort, rbuf[src, n0:n1]).astype(BF)
                gl[dst, n0:n1] = got[0:80]
                tl[dst, n0:n1] = got[80:160]
                if n1 <= 896:
                    gl[dst, 1920 + n0 : 1920 + n1] = got[160:240]
                elif n1 <= 1792:
                    tl[dst, 1024 + n0 : 1024 + n1] = got[160:240]
                else:
                    gl[dst, 2816:2880] = got[160:240, 0:64]
                    tl[dst, 2816:2880] = dot(got[160:240], down).astype(BF)[:, 0:64]

        @pl.loop(0, 11)
        def _(n):
            cols = pl.ds(pl.multiple_of(n * 256, 256), 256)
            proj[:, cols] = dot(tl[...], wgu[:, cols])

        proj[:, 2816:2880] = dot(tl[...], wgu[:, 2816:2880])

        @pl.loop(0, 5)
        def _(n):
            at = pl.ds(pl.multiple_of(n * 256, 256), 256)
            hg[:, at] = dot_nt(gl[...], wd[at, :])

        hg[:, 1280:1440] = dot_nt(gl[...], wd[1280:1440, :])

        @pl.loop(0, M // 16)
        def _(b):
            at = pl.ds(pl.multiple_of(b * 16, 16), 16)
            real = iota((16, WIDE), 1) < UNITS
            gate = proj[at, 0:WIDE]
            up1 = jnp.where(real, pltpu.roll(proj[at, 1408:2944], WIDE - 32, 1), 0.0) + 1.0
            hidden_grad = jnp.where(real, hg[at, :], 0.0)
            sig = 1.0 / (1.0 + jnp.exp(-swish_alpha * gate))
            act = gate * sig
            up_grad = hidden_grad * act
            term = jnp.sum(up_grad * up1, axis=1, keepdims=True)
            gate_grad = hidden_grad * up1 * sig * (1.0 + swish_alpha * gate * (1.0 - sig))
            moved = pltpu.roll(up_grad, 32, 1)
            pg[at, 0:1408] = gate_grad[:, 0:1408].astype(BF)
            pg[at, 1408:1536] = (gate_grad[:, 1408:1536] + moved[:, 0:128]).astype(BF)
            pg[at, 1536:2944] = moved[:, 128:1536].astype(BF)
            coarse = term.astype(BF).astype(F32)
            tile = iota((16, 128), 1)
            pair = jnp.where(tile == 0, coarse, jnp.where(tile == 1, term - coarse, 0.0)).astype(BF)
            group = b // 5
            pst[pl.ds(pl.multiple_of(group * 240 + 160 + (b - group * 5) * 16, 16), 16), 896:1024] = pair

        def put(part_of, lane, cols, value):
            value = value.astype(BF)
            for g in range(GROUPS):
                at = pl.ds(pl.multiple_of(g * 240 + part_of * 80, 16), 80)
                if cols == 64:
                    pst[at, 768:832] = value[g * 80 : g * 80 + 80]
                else:
                    pst[at, pl.ds(pl.multiple_of(lane, 256), cols)] = value[g * 80 : g * 80 + 80]

        @pl.loop(0, 11)
        def _(n):
            at = pl.ds(pl.multiple_of(n * 256, 256), 256)
            put(n // 4, (n % 4) * 256, 256, dot_nt(pg[:, 0:WIDTH], wgu[at, :]))

        put(2, 768, 64, dot_nt(pg[:, 0:WIDTH], wgu[2816:2880, :]))

        part, slot = wire_row(iota((256, 240), 0))
        target = part * 80 + (iota((256, 240), 0) >> 4) * 5 + slot - 1
        unsort = ((target == iota((256, 240), 1)) & (part < 3)).astype(F32).astype(BF)
        for g in range(GROUPS):
            dst = pl.ds(pl.multiple_of(c * ROWS + g * 256, 256), 256)
            for n in range(4):
                psend[dst, n * 256 : n * 256 + 256] = dot(
                    unsort, pst[g * 240 : g * 240 + 240, n * 256 : n * 256 + 256]
                ).astype(BF)

        @pl.when(c == 0)
        def _():
            pltpu.make_async_copy(psend.at[0:16], precv.at[0:16], prsem.at[0]).start()

        @pl.loop(jnp.where(c == 0, 1, 0), PER)
        def _(i):
            backward(c * PER + i, c).start()

    places_home = places_of(ids_ref[...])

    @pl.loop(0, CHUNKS)
    def _(c):
        rows = chunk_rows(c)
        pltpu.make_async_copy(psend.at[rows], precv.at[rows], prsem.at[c]).wait()
        place_of = c * PER + (iota((128, ROWS), 1) >> 4)
        spread = (iota((128, ROWS), 0) == place_of).astype(F32).astype(BF)
        slots = dot(slot_tp[...], spread)
        weights = dot(gate_tp[...], spread)
        part, slot = wire_row(iota((128, ROWS), 1))
        match = slots == slot.astype(F32)
        mix = jnp.concatenate(
            [jnp.where(match & (part == j), weights, 0.0).astype(BF) for j in range(3)], axis=0
        )
        for n in range(4):
            acc[:, n * 256 : n * 256 + 256] += dot(mix, precv[rows, n * 256 : n * 256 + 256])
        last = match & (part == 2)
        find = jnp.concatenate(
            [
                jnp.where(last & (places_home[:, k : k + 1] == place_of), 1.0, 0.0).astype(BF)
                for k in range(ROUTES)
            ],
            axis=0,
        )
        racc[...] += dot(find, precv[rows, 896:1024])

    out_ref[:, 0:1024] = acc[0:128, :].astype(BF)
    out_ref[:, 1024:2048] = acc[128:256, :].astype(BF)
    out_ref[:, 2048:2880] = acc[256:384, 0:832].astype(BF)
    terms = jnp.zeros((TOK, 128), F32)
    for k in range(ROUTES):
        found = racc[k * 128 : k * 128 + 128, :]
        terms = jnp.where(lanes == k, found[:, 0:1] + found[:, 1:2], terms)
    route_ref[...] = terms[:, 0:ROUTES]

    for c in range(CHUNKS):
        rows = pl.ds(16 if c == 0 else c * ROWS, ROWS - 16 if c == 0 else ROWS)
        pltpu.make_async_copy(sbuf.at[rows], rbuf.at[rows], ssem.at[c]).wait()
        pltpu.make_async_copy(psend.at[rows], precv.at[rows], pssem.at[c]).wait()


def shards(out_grad, tokens, expert_ids, gates, w_gate_up, w_down):
    vmem = pl.BlockSpec(memory_space=pltpu.VMEM)
    hbm = pl.BlockSpec(memory_space=pl.ANY)
    return pl.pallas_call(
        kernel,
        out_shape=(
            jax.ShapeDtypeStruct((TOK, WIDTH), BF),
            jax.ShapeDtypeStruct((TOK, ROUTES), F32),
        ),
        in_specs=[vmem, vmem, vmem, vmem, hbm, hbm],
        out_specs=(vmem, vmem),
        scratch_shapes=[
            pltpu.VMEM((WIDTH, WIDTH), BF),
            pltpu.VMEM((UNITS, WIDTH), BF),
            pltpu.VMEM((384, WIRE), BF),
            pltpu.VMEM((TOK, DEVICES), BF),
            pltpu.VMEM((TOK, DEVICES), BF),
            pltpu.VMEM((DEVICES * 16, WIRE), BF),
            pltpu.VMEM((DEVICES * 16, WIRE), BF),
            pltpu.VMEM((DEVICES * 16, BACK), BF),
            pltpu.VMEM((DEVICES * 16, BACK), BF),
            pltpu.VMEM((M, WIDTH), BF),
            pltpu.VMEM((M, WIDTH), BF),
            pltpu.VMEM((M, 2944), F32),
            pltpu.VMEM((M, WIDE), F32),
            pltpu.VMEM((M, 2944), BF),
            pltpu.VMEM((GROUPS * 240, BACK), BF),
            pltpu.VMEM((384, BACK), F32),
            pltpu.VMEM((ROUTES * TOK, 128), F32),
            pltpu.SemaphoreType.DMA((2,)),
            pltpu.SemaphoreType.DMA((CHUNKS,)),
            pltpu.SemaphoreType.DMA((CHUNKS,)),
            pltpu.SemaphoreType.DMA((CHUNKS,)),
            pltpu.SemaphoreType.DMA((CHUNKS,)),
        ],
        compiler_params=pltpu.CompilerParams(
            collective_id=0, has_side_effects=True, vmem_limit_bytes=63 * 2**20
        ),
    )(expert_ids, gates, out_grad, tokens, w_gate_up, w_down)


def solution(mesh):
    rows = P(("row", "col"), None)
    blocks = P(("row", "col"), None, None)
    return jax.shard_map(
        shards,
        mesh=mesh,
        in_specs=(rows, rows, rows, rows, blocks, blocks),
        out_specs=(rows, rows),
        check_vma=False,
    )
```

```python
import functools

import jax
import jax.numpy as jnp
from jax import lax
from jax.experimental import pallas as pl
from jax.experimental.pallas import tpu as pltpu
from jax.sharding import PartitionSpec as P

MESH = pl.DeviceIdType.MESH
BF = jnp.bfloat16
F32 = jnp.float32

swish_alpha = 1.702

DEVICES = 128
TOK = 128
ROUTES = 4
WIDTH = 2880
UNITS = 1440
WIRE = 1920
BACK = 1024
CHUNKS = 4
PER = DEVICES // CHUNKS
ROWS = PER * 16
GROUPS = PER // 16
M = PER * 5
WIDE = 1536


def dot(a, b):
    return jnp.dot(a, b, preferred_element_type=F32)


def dot_nt(a, b):
    return lax.dot_general(a, b, (((1,), (1,)), ((), ())), preferred_element_type=F32)


def iota(shape, axis):
    return lax.broadcasted_iota(jnp.int32, shape, axis)


def peer(place, sign):
    row, col = lax.axis_index("row"), lax.axis_index("col")
    step = place & 63
    a, b, c = step & 3, (step >> 2) & 3, step >> 4
    x = ((row >> 2) + sign * a) & 3
    y = ((row & 3) + sign * (a + b)) & 3
    z = ((col >> 1) + sign * (a + c)) & 3
    core = (col + (place >> 6)) & 1
    return (x * 4 + y, z * 2 + core)


def turn(i):
    return jnp.where(lax.axis_index("col") % 2 == 1, PER - 1 - i, i)


def places_of(experts):
    row, col = lax.axis_index("row"), lax.axis_index("col")
    dx = ((experts >> 5) - row // 4) & 3
    dy = ((experts >> 3) - row % 4) & 3
    dz = ((experts >> 1) - col // 2) & 3
    dc = (experts - col % 2) & 1
    return dc * 64 + ((dz - dx) & 3) * 16 + ((dy - dx) & 3) * 4 + dx


def wire_row(r):
    q = r & 15
    part = (q * 13) >> 6
    return part, q - 5 * part + 1


def kernel(
    ids_ref, gates_ref, grad_ref, tok_ref, wgu_hbm, wd_hbm,
    out_ref, route_ref,
    wgu, wd, xs, slot_pt, slot_tp, gate_tp, sbuf, rbuf, psend, precv, gl, tl, proj, hg, pg, pst, acc, terms,
    wsem, ssem, rsem, pssem, prsem,
):
    load_gu = pltpu.make_async_copy(wgu_hbm.at[0], wgu, wsem.at[0])
    load_d = pltpu.make_async_copy(wd_hbm.at[0], wd, wsem.at[1])
    load_gu.start()
    load_d.start()

    barrier = pltpu.get_barrier_semaphore()

    row, col = lax.axis_index("row"), lax.axis_index("col")
    for p in range(1, DEVICES):
        x, y = ((row >> 2) + (p >> 5)) & 3, ((row & 3) + (p >> 3)) & 3
        z, core = ((col >> 1) + (p >> 1)) & 3, (col + p) & 1
        pl.semaphore_signal(
            barrier, inc=1, device_id=(x * 4 + y, z * 2 + core), device_id_type=MESH
        )

    places = places_of(ids_ref[...])
    down = iota((DEVICES, TOK), 0)
    hits = [places[k : k + 1, :] == down for k in range(ROUTES)]
    chosen = jnp.zeros((DEVICES, TOK), F32)
    weight = jnp.zeros((DEVICES, TOK), F32)
    for k in range(ROUTES):
        chosen = jnp.where(hits[k], 1.0, chosen)
        weight = jnp.where(hits[k], gates_ref[k : k + 1, :], weight)
    earlier = (iota((TOK, TOK), 0) < iota((TOK, TOK), 1)).astype(F32).astype(BF)
    same = (iota((TOK, TOK), 0) == iota((TOK, TOK), 1)).astype(F32).astype(BF)
    slot_pt[...] = (chosen * (dot(chosen.astype(BF), earlier) + 1.0)).astype(BF)
    slot_tp[...] = dot_nt(same, slot_pt[...]).astype(BF)
    gate_tp[...] = dot_nt(same, weight.astype(BF)).astype(BF)

    for n in range(0, 1920, 384):
        xs[0:128, n : n + 384] = dot_nt(same, grad_ref[n : n + 384, :]).astype(BF)
        xs[128:256, n : n + 384] = dot_nt(same, tok_ref[n : n + 384, :]).astype(BF)
    for n, size in ((0, 384), (384, 512)):
        at = slice(1920 + n, 1920 + n + size)
        xs[256:384, n : n + size] = dot_nt(same, grad_ref[at, :]).astype(BF)
        xs[256:384, 896 + n : 896 + n + size] = dot_nt(same, tok_ref[at, :]).astype(BF)
    ends = jnp.concatenate([grad_ref[2816:2880, :], tok_ref[2816:2880, :]], axis=0)
    xs[256:384, 1792:1920] = dot_nt(same, ends).astype(BF)

    def pack(c):
        for g in range(ROWS // 256):
            base = c * ROWS + g * 256
            r = iota((256, 128), 0)
            spread = (iota((256, 128), 1) == c * PER + g * 16 + (r >> 4)).astype(F32).astype(BF)
            slots = dot(spread, slot_pt[...])
            part, slot = wire_row(r)
            match = slots == slot.astype(F32)
            pick = jnp.concatenate(
                [jnp.where(match & (part == j), 1.0, 0.0).astype(BF) for j in range(3)], axis=1
            )

            @pl.loop(0, 5)
            def _(n):
                cols = pl.ds(pl.multiple_of(n * 384, 128), 384)
                sbuf[pl.ds(pl.multiple_of(base, 256), 256), cols] = dot(pick, xs[:, cols]).astype(BF)

    def forward(p, c):
        rows = pl.ds(pl.multiple_of(p * 16, 16), 16)
        return pltpu.make_async_remote_copy(
            src_ref=sbuf.at[rows], dst_ref=rbuf.at[rows],
            send_sem=ssem.at[c], recv_sem=rsem.at[c],
            device_id=peer(p, 1), device_id_type=MESH,
        )

    def backward(p, c):
        rows = pl.ds(pl.multiple_of(p * 16, 16), 16)
        return pltpu.make_async_remote_copy(
            src_ref=psend.at[rows], dst_ref=precv.at[rows],
            send_sem=pssem.at[c], recv_sem=prsem.at[c],
            device_id=peer(p, -1), device_id_type=MESH,
        )

    pack(0)
    pl.semaphore_wait(barrier, DEVICES - 1)
    pltpu.make_async_copy(sbuf.at[0:16], rbuf.at[0:16], rsem.at[0]).start()

    @pl.loop(0, PER)
    def _(i):
        p = turn(i)

        @pl.when(p != 0)
        def _():
            forward(p, 0).start()

    @pl.loop(1, CHUNKS)
    def _(c):
        pack(c)

        @pl.loop(0, PER)
        def _(i):
            forward(c * PER + turn(i), c).start()

    pst[...] = jnp.zeros_like(pst)
    acc[...] = jnp.zeros_like(acc)
    load_gu.wait()
    load_d.wait()

    def chunk_rows(c):
        return pl.ds(pl.multiple_of(c * ROWS, 16), ROWS)

    @pl.loop(0, CHUNKS)
    def _(c):
        rows = chunk_rows(c)
        pltpu.make_async_copy(sbuf.at[rows], rbuf.at[rows], rsem.at[c]).wait()

        part, slot = wire_row(iota((240, 256), 1))
        target = part * 80 + (iota((240, 256), 1) >> 4) * 5 + slot - 1
        sort = ((target == iota((240, 256), 0)) & (part < 3)).astype(F32).astype(BF)
        shift = (iota((128, 128), 0) == iota((128, 128), 1) + 64).astype(F32).astype(BF)
        for g in range(GROUPS):
            src = pl.ds(pl.multiple_of(c * ROWS + g * 256, 256), 256)
            dst = slice(g * 80, g * 80 + 80)
            for n0, n1 in ((0, 256), (256, 512), (512, 896), (896, 1152), (1152, 1408), (1408, 1792), (1792, 1920)):
                got = dot(sort, rbuf[src, n0:n1]).astype(BF)
                gl[dst, n0:n1] = got[0:80]
                tl[dst, n0:n1] = got[80:160]
                if n1 <= 896:
                    gl[dst, 1920 + n0 : 1920 + n1] = got[160:240]
                elif n1 <= 1792:
                    tl[dst, 1024 + n0 : 1024 + n1] = got[160:240]
                else:
                    gl[dst, 2816:2880] = got[160:240, 0:64]
                    tl[dst, 2816:2880] = dot(got[160:240], shift).astype(BF)[:, 0:64]

        @pl.loop(0, 11)
        def _(n):
            cols = pl.ds(pl.multiple_of(n * 256, 256), 256)
            proj[:, cols] = dot(tl[...], wgu[:, cols])

        proj[:, 2816:2880] = dot(tl[...], wgu[:, 2816:2880])

        @pl.loop(0, 5)
        def _(n):
            at = pl.ds(pl.multiple_of(n * 256, 256), 256)
            hg[:, at] = dot_nt(gl[...], wd[at, :])

        hg[:, 1280:1440] = dot_nt(gl[...], wd[1280:1440, :])

        @pl.loop(0, M // 16)
        def _(b):
            at = pl.ds(pl.multiple_of(b * 16, 16), 16)
            real = iota((16, WIDE), 1) < UNITS
            gate = proj[at, 0:WIDE]
            up1 = jnp.where(real, pltpu.roll(proj[at, 1408:2944], WIDE - 32, 1), 0.0) + 1.0
            hidden_grad = jnp.where(real, hg[at, :], 0.0)
            sig = 1.0 / (1.0 + jnp.exp(-swish_alpha * gate))
            act = gate * sig
            up_grad = hidden_grad * act
            term = jnp.sum(up_grad * up1, axis=1, keepdims=True)
            gate_grad = hidden_grad * up1 * sig * (1.0 + swish_alpha * gate * (1.0 - sig))
            moved = pltpu.roll(up_grad, 32, 1)
            pg[at, 0:1408] = gate_grad[:, 0:1408].astype(BF)
            pg[at, 1408:1536] = (gate_grad[:, 1408:1536] + moved[:, 0:128]).astype(BF)
            pg[at, 1536:2944] = moved[:, 128:1536].astype(BF)
            coarse = term.astype(BF).astype(F32)
            tile = iota((16, 128), 1)
            pair = jnp.where(tile == 0, coarse, jnp.where(tile == 1, term - coarse, 0.0)).astype(BF)
            group = b // 5
            pst[pl.ds(pl.multiple_of(group * 240 + 160 + (b - group * 5) * 16, 16), 16), 896:1024] = pair

        def put(part_of, lane, cols, value):
            value = value.astype(BF)
            for g in range(GROUPS):
                at = pl.ds(pl.multiple_of(g * 240 + part_of * 80, 16), 80)
                if cols == 64:
                    pst[at, 768:832] = value[g * 80 : g * 80 + 80]
                else:
                    pst[at, pl.ds(pl.multiple_of(lane, 256), cols)] = value[g * 80 : g * 80 + 80]

        @pl.loop(0, 11)
        def _(n):
            at = pl.ds(pl.multiple_of(n * 256, 256), 256)
            put(n // 4, (n % 4) * 256, 256, dot_nt(pg[:, 0:WIDTH], wgu[at, :]))

        put(2, 768, 64, dot_nt(pg[:, 0:WIDTH], wgu[2816:2880, :]))

        part, slot = wire_row(iota((256, 240), 0))
        target = part * 80 + (iota((256, 240), 0) >> 4) * 5 + slot - 1
        unsort = ((target == iota((256, 240), 1)) & (part < 3)).astype(F32).astype(BF)
        for g in range(GROUPS):
            dst = pl.ds(pl.multiple_of(c * ROWS + g * 256, 256), 256)
            for n in range(4):
                psend[dst, n * 256 : n * 256 + 256] = dot(
                    unsort, pst[g * 240 : g * 240 + 240, n * 256 : n * 256 + 256]
                ).astype(BF)

        @pl.when(c == 0)
        def _():
            pltpu.make_async_copy(psend.at[0:16], precv.at[0:16], prsem.at[0]).start()

        @pl.loop(0, PER)
        def _(i):
            p = c * PER + turn(i)

            @pl.when(p != 0)
            def _():
                backward(p, c).start()

    @pl.loop(0, CHUNKS)
    def _(c):
        rows = chunk_rows(c)
        pltpu.make_async_copy(psend.at[rows], precv.at[rows], prsem.at[c]).wait()
        place_of = c * PER + (iota((128, ROWS), 1) >> 4)
        spread = (iota((128, ROWS), 0) == place_of).astype(F32).astype(BF)
        slots = dot(slot_tp[...], spread)
        weights = dot(gate_tp[...], spread)
        part, slot = wire_row(iota((128, ROWS), 1))
        match = slots == slot.astype(F32)
        mix = jnp.concatenate(
            [jnp.where(match & (part == j), weights, 0.0).astype(BF) for j in range(3)], axis=0
        )
        for n in range(4):
            acc[:, n * 256 : n * 256 + 256] += dot(mix, precv[rows, n * 256 : n * 256 + 256])
        out, at = iota((5 * PER, ROWS), 0), iota((5 * PER, ROWS), 1)
        number = out // PER
        find = ((out - number * PER) == (at >> 4)) & ((at & 15) == number + 10)
        found = dot(find.astype(F32).astype(BF), precv[rows, 896:1024])
        for i in range(5):
            terms[i, pl.ds(pl.multiple_of(c * PER, 16), PER), :] = found[i * PER : i * PER + PER]

    out_ref[:, 0:1024] = acc[0:128, :].astype(BF)
    out_ref[:, 1024:2048] = acc[128:256, :].astype(BF)
    out_ref[:, 2048:2880] = acc[256:384, 0:832].astype(BF)
    taken = slot_pt[...].astype(F32)
    value = jnp.zeros((DEVICES, TOK), F32)
    for i in range(5):
        value = jnp.where(taken == i + 1, terms[i, :, 0:1] + terms[i, :, 1:2], value)
    for k in range(ROUTES):
        hit = places[k : k + 1, :] == down
        route_ref[k : k + 1, :] = jnp.sum(jnp.where(hit, value, 0.0), axis=0, keepdims=True)

    for c in range(CHUNKS):
        rows = pl.ds(16 if c == 0 else c * ROWS, ROWS - 16 if c == 0 else ROWS)
        pltpu.make_async_copy(sbuf.at[rows], rbuf.at[rows], ssem.at[c]).wait()
        pltpu.make_async_copy(psend.at[rows], precv.at[rows], pssem.at[c]).wait()


def shards(out_grad, tokens, expert_ids, gates, w_gate_up, w_down):
    vmem = pl.BlockSpec(memory_space=pltpu.VMEM)
    hbm = pl.BlockSpec(memory_space=pl.ANY)
    input_grad, route_grad = pl.pallas_call(
        kernel,
        out_shape=(
            jax.ShapeDtypeStruct((TOK, WIDTH), BF),
            jax.ShapeDtypeStruct((ROUTES, TOK), F32),
        ),
        in_specs=[vmem, vmem, vmem, vmem, hbm, hbm],
        out_specs=(vmem, vmem),
        scratch_shapes=[
            pltpu.VMEM((WIDTH, WIDTH), BF),
            pltpu.VMEM((UNITS, WIDTH), BF),
            pltpu.VMEM((384, WIRE), BF),
            pltpu.VMEM((DEVICES, TOK), BF),
            pltpu.VMEM((TOK, DEVICES), BF),
            pltpu.VMEM((TOK, DEVICES), BF),
            pltpu.VMEM((DEVICES * 16, WIRE), BF),
            pltpu.VMEM((DEVICES * 16, WIRE), BF),
            pltpu.VMEM((DEVICES * 16, BACK), BF),
            pltpu.VMEM((DEVICES * 16, BACK), BF),
            pltpu.VMEM((M, WIDTH), BF),
            pltpu.VMEM((M, WIDTH), BF),
            pltpu.VMEM((M, 2944), F32),
            pltpu.VMEM((M, WIDE), F32),
            pltpu.VMEM((M, 2944), BF),
            pltpu.VMEM((GROUPS * 240, BACK), BF),
            pltpu.VMEM((384, BACK), F32),
            pltpu.VMEM((5, DEVICES, 128), F32),
            pltpu.SemaphoreType.DMA((2,)),
            pltpu.SemaphoreType.DMA((CHUNKS,)),
            pltpu.SemaphoreType.DMA((CHUNKS,)),
            pltpu.SemaphoreType.DMA((CHUNKS,)),
            pltpu.SemaphoreType.DMA((CHUNKS,)),
        ],
        compiler_params=pltpu.CompilerParams(
            collective_id=0, has_side_effects=True, vmem_limit_bytes=63 * 2**20
        ),
    )(expert_ids.T, gates.T, out_grad.T, tokens.T, w_gate_up, w_down)
    return input_grad, route_grad.T


def solution(mesh):
    rows = P(("row", "col"), None)
    blocks = P(("row", "col"), None, None)
    return jax.shard_map(
        shards,
        mesh=mesh,
        in_specs=(rows, rows, rows, rows, blocks, blocks),
        out_specs=(rows, rows),
        check_vma=False,
    )
```

```python
import functools

import jax
import jax.numpy as jnp
from jax import lax
from jax.experimental import pallas as pl
from jax.experimental.pallas import tpu as pltpu
from jax.sharding import PartitionSpec as P

MESH = pl.DeviceIdType.MESH
BF = jnp.bfloat16
F32 = jnp.float32

swish_alpha = 1.702

DEVICES = 128
TOK = 128
ROUTES = 4
WIDTH = 2880
UNITS = 1440
WIRE = 1920
BACK = 1024
CHUNKS = 4
PER = DEVICES // CHUNKS
ROWS = PER * 16
GROUPS = PER // 16
M = PER * 5
WIDE = 1536


def dot(a, b):
    return jnp.dot(a, b, preferred_element_type=F32)


def dot_nt(a, b):
    return lax.dot_general(a, b, (((1,), (1,)), ((), ())), preferred_element_type=F32)


def iota(shape, axis):
    return lax.broadcasted_iota(jnp.int32, shape, axis)


def peer(place, sign):
    row, col = lax.axis_index("row"), lax.axis_index("col")
    step = place & 63
    a, b, c = step & 3, (step >> 2) & 3, step >> 4
    x = ((row >> 2) + sign * a) & 3
    y = ((row & 3) + sign * (a + b)) & 3
    z = ((col >> 1) + sign * (a + c)) & 3
    core = (col + (place >> 6)) & 1
    return (x * 4 + y, z * 2 + core)


def turn(i):
    return jnp.where(lax.axis_index("col") % 2 == 1, PER - 1 - i, i)


def places_of(experts):
    row, col = lax.axis_index("row"), lax.axis_index("col")
    dx = ((experts >> 5) - row // 4) & 3
    dy = ((experts >> 3) - row % 4) & 3
    dz = ((experts >> 1) - col // 2) & 3
    dc = (experts - col % 2) & 1
    return dc * 64 + ((dz - dx) & 3) * 16 + ((dy - dx) & 3) * 4 + dx


def wire_row(r):
    q = r & 15
    part = (q * 13) >> 6
    return part, q - 5 * part + 1


def kernel(
    ids_ref, gates_ref, grad_ref, tok_ref, wgu_hbm, wd_hbm,
    out_ref, route_ref,
    wgu, wd, xs, slot_pt, slot_tp, gate_tp, sbuf, rbuf, psend, precv, gl, tl, proj, hg, pg, pst, acc, terms,
    wsem, ssem, rsem, pssem, prsem,
):
    load_gu = pltpu.make_async_copy(wgu_hbm.at[0], wgu, wsem.at[0])
    load_d = pltpu.make_async_copy(wd_hbm.at[0], wd, wsem.at[1])
    load_gu.start()
    load_d.start()

    barrier = pltpu.get_barrier_semaphore()

    row, col = lax.axis_index("row"), lax.axis_index("col")
    for p in range(1, DEVICES):
        x, y = ((row >> 2) + (p >> 5)) & 3, ((row & 3) + (p >> 3)) & 3
        z, core = ((col >> 1) + (p >> 1)) & 3, (col + p) & 1
        pl.semaphore_signal(
            barrier, inc=1, device_id=(x * 4 + y, z * 2 + core), device_id_type=MESH
        )

    places = places_of(ids_ref[...])
    down = iota((DEVICES, TOK), 0)
    hits = [places[k : k + 1, :] == down for k in range(ROUTES)]
    chosen = jnp.zeros((DEVICES, TOK), F32)
    weight = jnp.zeros((DEVICES, TOK), F32)
    for k in range(ROUTES):
        chosen = jnp.where(hits[k], 1.0, chosen)
        weight = jnp.where(hits[k], gates_ref[k : k + 1, :], weight)
    earlier = (iota((TOK, TOK), 0) < iota((TOK, TOK), 1)).astype(F32).astype(BF)
    same = (iota((TOK, TOK), 0) == iota((TOK, TOK), 1)).astype(F32).astype(BF)
    slot_pt[...] = (chosen * (dot(chosen.astype(BF), earlier) + 1.0)).astype(BF)
    slot_tp[...] = dot_nt(same, slot_pt[...]).astype(BF)
    gate_tp[...] = dot_nt(same, weight.astype(BF)).astype(BF)

    for n in range(0, 1920, 384):
        xs[0:128, n : n + 384] = dot_nt(same, grad_ref[n : n + 384, :]).astype(BF)
        xs[128:256, n : n + 384] = dot_nt(same, tok_ref[n : n + 384, :]).astype(BF)
    for n, size in ((0, 384), (384, 512)):
        at = slice(1920 + n, 1920 + n + size)
        xs[256:384, n : n + size] = dot_nt(same, grad_ref[at, :]).astype(BF)
        xs[256:384, 896 + n : 896 + n + size] = dot_nt(same, tok_ref[at, :]).astype(BF)
    ends = jnp.concatenate([grad_ref[2816:2880, :], tok_ref[2816:2880, :]], axis=0)
    xs[256:384, 1792:1920] = dot_nt(same, ends).astype(BF)

    def pack(c):
        for g in range(ROWS // 256):
            base = c * ROWS + g * 256
            r = iota((256, 128), 0)
            spread = (iota((256, 128), 1) == c * PER + g * 16 + (r >> 4)).astype(F32).astype(BF)
            slots = dot(spread, slot_pt[...])
            part, slot = wire_row(r)
            match = slots == slot.astype(F32)
            pick = jnp.concatenate(
                [jnp.where(match & (part == j), 1.0, 0.0).astype(BF) for j in range(3)], axis=1
            )

            @pl.loop(0, 5)
            def _(n):
                cols = pl.ds(pl.multiple_of(n * 384, 128), 384)
                sbuf[pl.ds(pl.multiple_of(base, 256), 256), cols] = dot(pick, xs[:, cols]).astype(BF)

    def forward(p, c):
        rows = pl.ds(pl.multiple_of(p * 16, 16), 16)
        return pltpu.make_async_remote_copy(
            src_ref=sbuf.at[rows], dst_ref=rbuf.at[rows],
            send_sem=ssem.at[c], recv_sem=rsem.at[c],
            device_id=peer(p, 1), device_id_type=MESH,
        )

    def backward(p, c):
        rows = pl.ds(pl.multiple_of(p * 16, 16), 16)
        return pltpu.make_async_remote_copy(
            src_ref=psend.at[rows], dst_ref=precv.at[rows],
            send_sem=pssem.at[c], recv_sem=prsem.at[c],
            device_id=peer(p, -1), device_id_type=MESH,
        )

    pack(0)
    pl.semaphore_wait(barrier, DEVICES - 1)
    pltpu.make_async_copy(sbuf.at[0:16], rbuf.at[0:16], rsem.at[0]).start()

    @pl.loop(0, PER)
    def _(i):
        p = turn(i)

        @pl.when(p != 0)
        def _():
            forward(p, 0).start()

    @pl.loop(1, CHUNKS)
    def _(c):
        pack(c)

        @pl.loop(0, PER)
        def _(i):
            forward(c * PER + turn(i), c).start()

    pst[...] = jnp.zeros_like(pst)
    acc[...] = jnp.zeros_like(acc)
    load_gu.wait()
    load_d.wait()

    def chunk_rows(c):
        return pl.ds(pl.multiple_of(c * ROWS, 16), ROWS)

    @pl.loop(0, CHUNKS)
    def _(c):
        rows = chunk_rows(c)
        pltpu.make_async_copy(sbuf.at[rows], rbuf.at[rows], rsem.at[c]).wait()

        part, slot = wire_row(iota((240, 256), 1))
        target = part * 80 + (iota((240, 256), 1) >> 4) * 5 + slot - 1
        sort = ((target == iota((240, 256), 0)) & (part < 3)).astype(F32).astype(BF)
        shift = (iota((128, 128), 0) == iota((128, 128), 1) + 64).astype(F32).astype(BF)
        for g in range(GROUPS):
            src = pl.ds(pl.multiple_of(c * ROWS + g * 256, 256), 256)
            dst = slice(g * 80, g * 80 + 80)
            for n0, n1 in ((0, 256), (256, 512), (512, 896), (896, 1152), (1152, 1408), (1408, 1792), (1792, 1920)):
                got = dot(sort, rbuf[src, n0:n1]).astype(BF)
                gl[dst, n0:n1] = got[0:80]
                tl[dst, n0:n1] = got[80:160]
                if n1 <= 896:
                    gl[dst, 1920 + n0 : 1920 + n1] = got[160:240]
                elif n1 <= 1792:
                    tl[dst, 1024 + n0 : 1024 + n1] = got[160:240]
                else:
                    gl[dst, 2816:2880] = got[160:240, 0:64]
                    tl[dst, 2816:2880] = dot(got[160:240], shift).astype(BF)[:, 0:64]

        @pl.loop(0, 5)
        def _(n):
            cols = pl.ds(pl.multiple_of(n * 512, 512), 512)
            proj[:, cols] = dot(tl[...], wgu[:, cols])

        proj[:, 2560:2880] = dot(tl[...], wgu[:, 2560:2880])

        @pl.loop(0, 2)
        def _(n):
            at = pl.ds(pl.multiple_of(n * 512, 512), 512)
            hg[:, at] = dot_nt(gl[...], wd[at, :])

        hg[:, 1024:1440] = dot_nt(gl[...], wd[1024:1440, :])

        @pl.loop(0, M // 16)
        def _(b):
            at = pl.ds(pl.multiple_of(b * 16, 16), 16)
            real = iota((16, WIDE), 1) < UNITS
            gate = proj[at, 0:WIDE]
            up1 = jnp.where(real, pltpu.roll(proj[at, 1408:2944], WIDE - 32, 1), 0.0) + 1.0
            hidden_grad = jnp.where(real, hg[at, :], 0.0)
            sig = 1.0 / (1.0 + jnp.exp(-swish_alpha * gate))
            act = gate * sig
            up_grad = hidden_grad * act
            term = jnp.sum(up_grad * up1, axis=1, keepdims=True)
            gate_grad = hidden_grad * up1 * sig * (1.0 + swish_alpha * gate * (1.0 - sig))
            moved = pltpu.roll(up_grad, 32, 1)
            pg[at, 0:1408] = gate_grad[:, 0:1408].astype(BF)
            pg[at, 1408:1536] = (gate_grad[:, 1408:1536] + moved[:, 0:128]).astype(BF)
            pg[at, 1536:2944] = moved[:, 128:1536].astype(BF)
            coarse = term.astype(BF).astype(F32)
            tile = iota((16, 128), 1)
            pair = jnp.where(tile == 0, coarse, jnp.where(tile == 1, term - coarse, 0.0)).astype(BF)
            group = b // 5
            pst[pl.ds(pl.multiple_of(group * 240 + 160 + (b - group * 5) * 16, 16), 16), 896:1024] = pair

        def put(part_of, lane, cols, value):
            value = value.astype(BF)
            for g in range(GROUPS):
                at = pl.ds(pl.multiple_of(g * 240 + part_of * 80, 16), 80)
                if cols == 320:
                    pst[at, 512:832] = value[g * 80 : g * 80 + 80]
                else:
                    pst[at, pl.ds(pl.multiple_of(lane, 512), cols)] = value[g * 80 : g * 80 + 80]

        @pl.loop(0, 5)
        def _(n):
            at = pl.ds(pl.multiple_of(n * 512, 512), 512)
            put(n // 2, (n % 2) * 512, 512, dot_nt(pg[:, 0:WIDTH], wgu[at, :]))

        put(2, 512, 320, dot_nt(pg[:, 0:WIDTH], wgu[2560:2880, :]))

        part, slot = wire_row(iota((256, 240), 0))
        target = part * 80 + (iota((256, 240), 0) >> 4) * 5 + slot - 1
        unsort = ((target == iota((256, 240), 1)) & (part < 3)).astype(F32).astype(BF)
        for g in range(GROUPS):
            dst = pl.ds(pl.multiple_of(c * ROWS + g * 256, 256), 256)
            for n in range(4):
                psend[dst, n * 256 : n * 256 + 256] = dot(
                    unsort, pst[g * 240 : g * 240 + 240, n * 256 : n * 256 + 256]
                ).astype(BF)

        @pl.when(c == 0)
        def _():
            pltpu.make_async_copy(psend.at[0:16], precv.at[0:16], prsem.at[0]).start()

        @pl.loop(0, PER)
        def _(i):
            p = c * PER + turn(i)

            @pl.when(p != 0)
            def _():
                backward(p, c).start()

    @pl.loop(0, CHUNKS)
    def _(c):
        rows = chunk_rows(c)
        pltpu.make_async_copy(psend.at[rows], precv.at[rows], prsem.at[c]).wait()
        place_of = c * PER + (iota((128, ROWS), 1) >> 4)
        spread = (iota((128, ROWS), 0) == place_of).astype(F32).astype(BF)
        slots = dot(slot_tp[...], spread)
        weights = dot(gate_tp[...], spread)
        part, slot = wire_row(iota((128, ROWS), 1))
        match = slots == slot.astype(F32)
        mix = jnp.concatenate(
            [jnp.where(match & (part == j), weights, 0.0).astype(BF) for j in range(3)], axis=0
        )
        for n in range(4):
            acc[:, n * 256 : n * 256 + 256] += dot(mix, precv[rows, n * 256 : n * 256 + 256])
        out, at = iota((5 * PER, ROWS), 0), iota((5 * PER, ROWS), 1)
        number = out // PER
        find = ((out - number * PER) == (at >> 4)) & ((at & 15) == number + 10)
        found = dot(find.astype(F32).astype(BF), precv[rows, 896:1024])
        for i in range(5):
            terms[i, pl.ds(pl.multiple_of(c * PER, 16), PER), :] = found[i * PER : i * PER + PER]

    out_ref[:, 0:1024] = acc[0:128, :].astype(BF)
    out_ref[:, 1024:2048] = acc[128:256, :].astype(BF)
    out_ref[:, 2048:2880] = acc[256:384, 0:832].astype(BF)
    taken = slot_pt[...].astype(F32)
    value = jnp.zeros((DEVICES, TOK), F32)
    for i in range(5):
        value = jnp.where(taken == i + 1, terms[i, :, 0:1] + terms[i, :, 1:2], value)
    for k in range(ROUTES):
        hit = places[k : k + 1, :] == down
        route_ref[k : k + 1, :] = jnp.sum(jnp.where(hit, value, 0.0), axis=0, keepdims=True)

    for c in range(CHUNKS):
        rows = pl.ds(16 if c == 0 else c * ROWS, ROWS - 16 if c == 0 else ROWS)
        pltpu.make_async_copy(sbuf.at[rows], rbuf.at[rows], ssem.at[c]).wait()
        pltpu.make_async_copy(psend.at[rows], precv.at[rows], pssem.at[c]).wait()


def shards(out_grad, tokens, expert_ids, gates, w_gate_up, w_down):
    vmem = pl.BlockSpec(memory_space=pltpu.VMEM)
    hbm = pl.BlockSpec(memory_space=pl.ANY)
    input_grad, route_grad = pl.pallas_call(
        kernel,
        out_shape=(
            jax.ShapeDtypeStruct((TOK, WIDTH), BF),
            jax.ShapeDtypeStruct((ROUTES, TOK), F32),
        ),
        in_specs=[vmem, vmem, vmem, vmem, hbm, hbm],
        out_specs=(vmem, vmem),
        scratch_shapes=[
            pltpu.VMEM((WIDTH, WIDTH), BF),
            pltpu.VMEM((UNITS, WIDTH), BF),
            pltpu.VMEM((384, WIRE), BF),
            pltpu.VMEM((DEVICES, TOK), BF),
            pltpu.VMEM((TOK, DEVICES), BF),
            pltpu.VMEM((TOK, DEVICES), BF),
            pltpu.VMEM((DEVICES * 16, WIRE), BF),
            pltpu.VMEM((DEVICES * 16, WIRE), BF),
            pltpu.VMEM((DEVICES * 16, BACK), BF),
            pltpu.VMEM((DEVICES * 16, BACK), BF),
            pltpu.VMEM((M, WIDTH), BF),
            pltpu.VMEM((M, WIDTH), BF),
            pltpu.VMEM((M, 2944), F32),
            pltpu.VMEM((M, WIDE), F32),
            pltpu.VMEM((M, 2944), BF),
            pltpu.VMEM((GROUPS * 240, BACK), BF),
            pltpu.VMEM((384, BACK), F32),
            pltpu.VMEM((5, DEVICES, 128), F32),
            pltpu.SemaphoreType.DMA((2,)),
            pltpu.SemaphoreType.DMA((CHUNKS,)),
            pltpu.SemaphoreType.DMA((CHUNKS,)),
            pltpu.SemaphoreType.DMA((CHUNKS,)),
            pltpu.SemaphoreType.DMA((CHUNKS,)),
        ],
        compiler_params=pltpu.CompilerParams(
            collective_id=0, has_side_effects=True, vmem_limit_bytes=63 * 2**20
        ),
    )(expert_ids.T, gates.T, out_grad.T, tokens.T, w_gate_up, w_down)
    return input_grad, route_grad.T


def solution(mesh):
    rows = P(("row", "col"), None)
    blocks = P(("row", "col"), None, None)
    return jax.shard_map(
        shards,
        mesh=mesh,
        in_specs=(rows, rows, rows, rows, blocks, blocks),
        out_specs=(rows, rows),
        check_vma=False,
    )
```

```python
import functools

import jax
import jax.numpy as jnp
from jax import lax
from jax.experimental import pallas as pl
from jax.experimental.pallas import tpu as pltpu
from jax.sharding import PartitionSpec as P

MESH = pl.DeviceIdType.MESH
BF = jnp.bfloat16
F32 = jnp.float32

swish_alpha = 1.702

DEVICES = 128
TOK = 128
ROUTES = 4
WIDTH = 2880
UNITS = 1440
WIRE = 1920
BACK = 1024
CHUNKS = 4
PER = DEVICES // CHUNKS
ROWS = PER * 16
GROUPS = PER // 16
M = PER * 5
WIDE = 1536


def dot(a, b):
    return jnp.dot(a, b, preferred_element_type=F32)


def dot_nt(a, b):
    return lax.dot_general(a, b, (((1,), (1,)), ((), ())), preferred_element_type=F32)


def iota(shape, axis):
    return lax.broadcasted_iota(jnp.int32, shape, axis)


def peer(place, sign):
    row, col = lax.axis_index("row"), lax.axis_index("col")
    step = place & 63
    a, b, c = step & 3, (step >> 2) & 3, step >> 4
    x = ((row >> 2) + sign * a) & 3
    y = ((row & 3) + sign * (a + b)) & 3
    z = ((col >> 1) + sign * (a + c)) & 3
    core = (col + (place >> 6)) & 1
    return (x * 4 + y, z * 2 + core)


def turn(i):
    return jnp.where(lax.axis_index("col") % 2 == 1, PER - 1 - i, i)


def places_of(experts):
    row, col = lax.axis_index("row"), lax.axis_index("col")
    dx = ((experts >> 5) - row // 4) & 3
    dy = ((experts >> 3) - row % 4) & 3
    dz = ((experts >> 1) - col // 2) & 3
    dc = (experts - col % 2) & 1
    return dc * 64 + ((dz - dx) & 3) * 16 + ((dy - dx) & 3) * 4 + dx


def wire_row(r):
    q = r & 15
    part = (q * 13) >> 6
    return part, q - 5 * part + 1


def kernel(
    ids_ref, gates_ref, grad_ref, tok_ref, wgu_hbm, wd_hbm,
    out_ref, route_ref,
    wgu, wd, xs, slot_pt, slot_tp, gate_tp, sbuf, rbuf, psend, precv, gl, tl, proj, hg, pg, pst, acc, terms,
    wsem, ssem, rsem, pssem, prsem,
):
    load_gu = pltpu.make_async_copy(wgu_hbm.at[0], wgu, wsem.at[0])
    load_d = pltpu.make_async_copy(wd_hbm.at[0], wd, wsem.at[1])
    load_gu.start()
    load_d.start()

    barrier = pltpu.get_barrier_semaphore()

    row, col = lax.axis_index("row"), lax.axis_index("col")
    for p in range(1, DEVICES):
        x, y = ((row >> 2) + (p >> 5)) & 3, ((row & 3) + (p >> 3)) & 3
        z, core = ((col >> 1) + (p >> 1)) & 3, (col + p) & 1
        pl.semaphore_signal(
            barrier, inc=1, device_id=(x * 4 + y, z * 2 + core), device_id_type=MESH
        )

    places = places_of(ids_ref[...])
    down = iota((DEVICES, TOK), 0)
    hits = [places[k : k + 1, :] == down for k in range(ROUTES)]
    chosen = jnp.zeros((DEVICES, TOK), F32)
    weight = jnp.zeros((DEVICES, TOK), F32)
    for k in range(ROUTES):
        chosen = jnp.where(hits[k], 1.0, chosen)
        weight = jnp.where(hits[k], gates_ref[k : k + 1, :], weight)
    earlier = (iota((TOK, TOK), 0) < iota((TOK, TOK), 1)).astype(F32).astype(BF)
    same = (iota((TOK, TOK), 0) == iota((TOK, TOK), 1)).astype(F32).astype(BF)
    slot_pt[...] = (chosen * (dot(chosen.astype(BF), earlier) + 1.0)).astype(BF)
    slot_tp[...] = dot_nt(same, slot_pt[...]).astype(BF)
    gate_tp[...] = dot_nt(same, weight.astype(BF)).astype(BF)

    for n in range(0, 1920, 384):
        xs[0:128, n : n + 384] = dot_nt(same, grad_ref[n : n + 384, :]).astype(BF)
        xs[128:256, n : n + 384] = dot_nt(same, tok_ref[n : n + 384, :]).astype(BF)
    for n, size in ((0, 384), (384, 512)):
        at = slice(1920 + n, 1920 + n + size)
        xs[256:384, n : n + size] = dot_nt(same, grad_ref[at, :]).astype(BF)
        xs[256:384, 896 + n : 896 + n + size] = dot_nt(same, tok_ref[at, :]).astype(BF)
    ends = jnp.concatenate([grad_ref[2816:2880, :], tok_ref[2816:2880, :]], axis=0)
    xs[256:384, 1792:1920] = dot_nt(same, ends).astype(BF)

    def pack(c):
        for g in range(ROWS // 256):
            base = c * ROWS + g * 256
            r = iota((256, 128), 0)
            spread = (iota((256, 128), 1) == c * PER + g * 16 + (r >> 4)).astype(F32).astype(BF)
            slots = dot(spread, slot_pt[...])
            part, slot = wire_row(r)
            match = slots == slot.astype(F32)
            pick = jnp.concatenate(
                [jnp.where(match & (part == j), 1.0, 0.0).astype(BF) for j in range(3)], axis=1
            )

            @pl.loop(0, 5)
            def _(n):
                cols = pl.ds(pl.multiple_of(n * 384, 128), 384)
                sbuf[pl.ds(pl.multiple_of(base, 256), 256), cols] = dot(pick, xs[:, cols]).astype(BF)

    def forward(p, c):
        rows = pl.ds(pl.multiple_of(p * 16, 16), 16)
        return pltpu.make_async_remote_copy(
            src_ref=sbuf.at[rows], dst_ref=rbuf.at[rows],
            send_sem=ssem.at[c], recv_sem=rsem.at[c],
            device_id=peer(p, 1), device_id_type=MESH,
        )

    def backward(p, c, half):
        rows = pl.ds(pl.multiple_of(p * 16, 16), 16)
        cols = slice(half * 512, half * 512 + 512)
        return pltpu.make_async_remote_copy(
            src_ref=psend.at[rows, cols], dst_ref=precv.at[rows, cols],
            send_sem=pssem.at[c], recv_sem=prsem.at[c],
            device_id=peer(p, -1), device_id_type=MESH,
        )

    pack(0)
    pl.semaphore_wait(barrier, DEVICES - 1)
    pltpu.make_async_copy(sbuf.at[0:16], rbuf.at[0:16], rsem.at[0]).start()

    @pl.loop(0, PER)
    def _(i):
        p = turn(i)

        @pl.when(p != 0)
        def _():
            forward(p, 0).start()

    @pl.loop(1, CHUNKS)
    def _(c):
        pack(c)

        @pl.loop(0, PER)
        def _(i):
            forward(c * PER + turn(i), c).start()

    pst[...] = jnp.zeros_like(pst)
    acc[...] = jnp.zeros_like(acc)
    load_gu.wait()
    load_d.wait()

    def chunk_rows(c):
        return pl.ds(pl.multiple_of(c * ROWS, 16), ROWS)

    @pl.loop(0, CHUNKS)
    def _(c):
        rows = chunk_rows(c)
        pltpu.make_async_copy(sbuf.at[rows], rbuf.at[rows], rsem.at[c]).wait()

        part, slot = wire_row(iota((240, 256), 1))
        target = part * 80 + (iota((240, 256), 1) >> 4) * 5 + slot - 1
        sort = ((target == iota((240, 256), 0)) & (part < 3)).astype(F32).astype(BF)
        shift = (iota((128, 128), 0) == iota((128, 128), 1) + 64).astype(F32).astype(BF)
        for g in range(GROUPS):
            src = pl.ds(pl.multiple_of(c * ROWS + g * 256, 256), 256)
            dst = slice(g * 80, g * 80 + 80)
            for n0, n1 in ((0, 256), (256, 512), (512, 896), (896, 1152), (1152, 1408), (1408, 1792), (1792, 1920)):
                got = dot(sort, rbuf[src, n0:n1]).astype(BF)
                gl[dst, n0:n1] = got[0:80]
                tl[dst, n0:n1] = got[80:160]
                if n1 <= 896:
                    gl[dst, 1920 + n0 : 1920 + n1] = got[160:240]
                elif n1 <= 1792:
                    tl[dst, 1024 + n0 : 1024 + n1] = got[160:240]
                else:
                    gl[dst, 2816:2880] = got[160:240, 0:64]
                    tl[dst, 2816:2880] = dot(got[160:240], shift).astype(BF)[:, 0:64]

        @pl.loop(0, 5)
        def _(n):
            cols = pl.ds(pl.multiple_of(n * 512, 512), 512)
            proj[:, cols] = dot(tl[...], wgu[:, cols])

        proj[:, 2560:2880] = dot(tl[...], wgu[:, 2560:2880])

        @pl.loop(0, 2)
        def _(n):
            at = pl.ds(pl.multiple_of(n * 512, 512), 512)
            hg[:, at] = dot_nt(gl[...], wd[at, :])

        hg[:, 1024:1440] = dot_nt(gl[...], wd[1024:1440, :])

        @pl.loop(0, M // 16)
        def _(b):
            at = pl.ds(pl.multiple_of(b * 16, 16), 16)
            real = iota((16, WIDE), 1) < UNITS
            gate = proj[at, 0:WIDE]
            up1 = jnp.where(real, pltpu.roll(proj[at, 1408:2944], WIDE - 32, 1), 0.0) + 1.0
            hidden_grad = jnp.where(real, hg[at, :], 0.0)
            sig = 1.0 / (1.0 + jnp.exp(-swish_alpha * gate))
            act = gate * sig
            up_grad = hidden_grad * act
            term = jnp.sum(up_grad * up1, axis=1, keepdims=True)
            gate_grad = hidden_grad * up1 * sig * (1.0 + swish_alpha * gate * (1.0 - sig))
            moved = pltpu.roll(up_grad, 32, 1)
            pg[at, 0:1408] = gate_grad[:, 0:1408].astype(BF)
            pg[at, 1408:1536] = (gate_grad[:, 1408:1536] + moved[:, 0:128]).astype(BF)
            pg[at, 1536:2944] = moved[:, 128:1536].astype(BF)
            coarse = term.astype(BF).astype(F32)
            tile = iota((16, 128), 1)
            pair = jnp.where(tile == 0, coarse, jnp.where(tile == 1, term - coarse, 0.0)).astype(BF)
            group = b // 5
            pst[pl.ds(pl.multiple_of(group * 240 + 160 + (b - group * 5) * 16, 16), 16), 896:1024] = pair

        def put(part_of, lane, cols, value):
            value = value.astype(BF)
            for g in range(GROUPS):
                at = pl.ds(pl.multiple_of(g * 240 + part_of * 80, 16), 80)
                if cols == 320:
                    pst[at, 512:832] = value[g * 80 : g * 80 + 80]
                else:
                    pst[at, lane : lane + cols] = value[g * 80 : g * 80 + 80]

        part, slot = wire_row(iota((256, 240), 0))
        target = part * 80 + (iota((256, 240), 0) >> 4) * 5 + slot - 1
        unsort = ((target == iota((256, 240), 1)) & (part < 3)).astype(F32).astype(BF)

        for half in range(2):

            @pl.loop(0, 3 - half)
            def _(n):
                at = pl.ds(pl.multiple_of(n * 1024 + half * 512, 512), 512)
                put(n, half * 512, 512, dot_nt(pg[:, 0:WIDTH], wgu[at, :]))

            if half == 1:
                put(2, 512, 320, dot_nt(pg[:, 0:WIDTH], wgu[2560:2880, :]))
            for g in range(GROUPS):
                dst = pl.ds(pl.multiple_of(c * ROWS + g * 256, 256), 256)
                for n in range(2 * half, 2 * half + 2):
                    psend[dst, n * 256 : n * 256 + 256] = dot(
                        unsort, pst[g * 240 : g * 240 + 240, n * 256 : n * 256 + 256]
                    ).astype(BF)

            @pl.loop(0, PER)
            def _(i):
                p = c * PER + turn(i)

                @pl.when(p != 0)
                def _():
                    backward(p, c, half).start()

        @pl.when(c == 0)
        def _():
            pltpu.make_async_copy(psend.at[0:16], precv.at[0:16], prsem.at[0]).start()

    @pl.loop(0, CHUNKS)
    def _(c):
        rows = chunk_rows(c)
        pltpu.make_async_copy(psend.at[rows], precv.at[rows], prsem.at[c]).wait()
        place_of = c * PER + (iota((128, ROWS), 1) >> 4)
        spread = (iota((128, ROWS), 0) == place_of).astype(F32).astype(BF)
        slots = dot(slot_tp[...], spread)
        weights = dot(gate_tp[...], spread)
        part, slot = wire_row(iota((128, ROWS), 1))
        match = slots == slot.astype(F32)
        mix = jnp.concatenate(
            [jnp.where(match & (part == j), weights, 0.0).astype(BF) for j in range(3)], axis=0
        )
        for n in range(4):
            acc[:, n * 256 : n * 256 + 256] += dot(mix, precv[rows, n * 256 : n * 256 + 256])
        out, at = iota((5 * PER, ROWS), 0), iota((5 * PER, ROWS), 1)
        number = out // PER
        find = ((out - number * PER) == (at >> 4)) & ((at & 15) == number + 10)
        found = dot(find.astype(F32).astype(BF), precv[rows, 896:1024])
        for i in range(5):
            terms[i, pl.ds(pl.multiple_of(c * PER, 16), PER), :] = found[i * PER : i * PER + PER]

    out_ref[:, 0:1024] = acc[0:128, :].astype(BF)
    out_ref[:, 1024:2048] = acc[128:256, :].astype(BF)
    out_ref[:, 2048:2880] = acc[256:384, 0:832].astype(BF)
    taken = slot_pt[...].astype(F32)
    value = jnp.zeros((DEVICES, TOK), F32)
    for i in range(5):
        value = jnp.where(taken == i + 1, terms[i, :, 0:1] + terms[i, :, 1:2], value)
    for k in range(ROUTES):
        hit = places[k : k + 1, :] == down
        route_ref[k : k + 1, :] = jnp.sum(jnp.where(hit, value, 0.0), axis=0, keepdims=True)

    for c in range(CHUNKS):
        rows = pl.ds(16 if c == 0 else c * ROWS, ROWS - 16 if c == 0 else ROWS)
        pltpu.make_async_copy(sbuf.at[rows], rbuf.at[rows], ssem.at[c]).wait()
        pltpu.make_async_copy(psend.at[rows], precv.at[rows], pssem.at[c]).wait()


def shards(out_grad, tokens, expert_ids, gates, w_gate_up, w_down):
    vmem = pl.BlockSpec(memory_space=pltpu.VMEM)
    hbm = pl.BlockSpec(memory_space=pl.ANY)
    input_grad, route_grad = pl.pallas_call(
        kernel,
        out_shape=(
            jax.ShapeDtypeStruct((TOK, WIDTH), BF),
            jax.ShapeDtypeStruct((ROUTES, TOK), F32),
        ),
        in_specs=[vmem, vmem, vmem, vmem, hbm, hbm],
        out_specs=(vmem, vmem),
        scratch_shapes=[
            pltpu.VMEM((WIDTH, WIDTH), BF),
            pltpu.VMEM((UNITS, WIDTH), BF),
            pltpu.VMEM((384, WIRE), BF),
            pltpu.VMEM((DEVICES, TOK), BF),
            pltpu.VMEM((TOK, DEVICES), BF),
            pltpu.VMEM((TOK, DEVICES), BF),
            pltpu.VMEM((DEVICES * 16, WIRE), BF),
            pltpu.VMEM((DEVICES * 16, WIRE), BF),
            pltpu.VMEM((DEVICES * 16, BACK), BF),
            pltpu.VMEM((DEVICES * 16, BACK), BF),
            pltpu.VMEM((M, WIDTH), BF),
            pltpu.VMEM((M, WIDTH), BF),
            pltpu.VMEM((M, 2944), F32),
            pltpu.VMEM((M, WIDE), F32),
            pltpu.VMEM((M, 2944), BF),
            pltpu.VMEM((GROUPS * 240, BACK), BF),
            pltpu.VMEM((384, BACK), F32),
            pltpu.VMEM((5, DEVICES, 128), F32),
            pltpu.SemaphoreType.DMA((2,)),
            pltpu.SemaphoreType.DMA((CHUNKS,)),
            pltpu.SemaphoreType.DMA((CHUNKS,)),
            pltpu.SemaphoreType.DMA((CHUNKS,)),
            pltpu.SemaphoreType.DMA((CHUNKS,)),
        ],
        compiler_params=pltpu.CompilerParams(
            collective_id=0, has_side_effects=True, vmem_limit_bytes=63 * 2**20
        ),
    )(expert_ids.T, gates.T, out_grad.T, tokens.T, w_gate_up, w_down)
    return input_grad, route_grad.T


def solution(mesh):
    rows = P(("row", "col"), None)
    blocks = P(("row", "col"), None, None)
    return jax.shard_map(
        shards,
        mesh=mesh,
        in_specs=(rows, rows, rows, rows, blocks, blocks),
        out_specs=(rows, rows),
        check_vma=False,
    )
```
